256 devices in a mesh: grp: 8 (over z), seq: 32 (over y, x, core).
Axes of the slice: x: 4, y: 4, z: 8, core: 2. Of those that a mesh axis runs over, the one named last changes fastest.
Arguments:
- queries: bfloat16 [28, 4096, 2048], P(None, ('grp', 'seq')), parts along dimension 1, may hold values from -16 to 16
- keys: bfloat16 [28, 4096, 2048], P(None, ('grp', 'seq')), parts along dimension 1, may hold values from -16 to 16
- values: bfloat16 [28, 4096, 2048], P(None, ('grp', 'seq')), parts along dimension 1, may hold values from -6 to 6
- cotangent: bfloat16 [28, 4096, 2048], P(None, ('grp', 'seq')), parts along dimension 1, may hold values from -6 to 6
- lengths: int32 [384], P('grp'), parts along dimension 0, may hold values from 16 to 512, as said below
Outputs:
- grad_queries: bfloat16 [28, 4096, 2048], P(None, ('grp', 'seq')), parts along dimension 1
- grad_keys: bfloat16 [28, 4096, 2048], P(None, ('grp', 'seq')), parts along dimension 1
- grad_values: bfloat16 [28, 4096, 2048], P(None, ('grp', 'seq')), parts along dimension 1
The draws below stay inside these ranges and needn't reach their ends.
There are 8 independent parts, one for each index of `grp`. The reference program is written for one: setup_inputs(seed, part) draws one part's arguments, and reference() takes and returns one part's arrays. A program takes and returns all parts, laid end to end along the dimension named above; each array names one. Nothing has to cross between parts.
Inputs may be any that keep to these rules, and one draw needn't show every extreme that they name: Every length is a multiple of 16; the lengths sum to 14336.
All inputs are finite; a program needn't handle non-finite values.
Results may differ from the reference program's by a relative error of at most 0.0093.
Values may be sent and summed in bfloat16 or wider, within the bound.
A program may use at most 192 MiB of HBM per device.

```python
import math
import jax
import jax.numpy as jnp
from jax import lax

HEADS = 16
HEAD_DIM = 128
TILE = 16
ROUNDS = 28
BAND = 512
TOKENS = 14336
DOCS = 48
WIDTH = 2048
N_SEQ = 32


def draw_queries(key, part):
    key = jax.random.fold_in(key, 21)
    drawn = jnp.clip(jax.random.normal(key, (ROUNDS, BAND, WIDTH), jnp.float32), -4.0, 4.0)
    return drawn.astype(jnp.bfloat16)


def draw_keys(key, part):
    key = jax.random.fold_in(key, 22)
    drawn = jnp.clip(jax.random.normal(key, (ROUNDS, BAND, WIDTH), jnp.float32), -4.0, 4.0)
    return drawn.astype(jnp.bfloat16)


def draw_lengths(key, part):
    key = jax.random.fold_in(key, 11)
    key_pairs, key_swing, key_longest = jax.random.split(key, 3)
    other_docs = DOCS - 1
    spare_tiles = ROUNDS * N_SEQ - N_SEQ
    even_share = spare_tiles // other_docs
    leftover = spare_tiles - even_share * other_docs
    swing_most = min(N_SEQ - even_share - 1, even_share - 1)
    position = jnp.arange(other_docs, dtype=jnp.int32)
    tile_counts = even_share + (position < leftover).astype(jnp.int32)
    shuffled = jax.random.permutation(key_pairs, other_docs).astype(jnp.int32)
    pair_count = other_docs // 2
    swing = jax.random.randint(key_swing, (pair_count,), -swing_most, swing_most + 1).astype(jnp.int32)
    adjusted = jnp.zeros((other_docs,), jnp.int32)
    adjusted = adjusted.at[shuffled[0:2 * pair_count:2]].add(swing)
    adjusted = adjusted.at[shuffled[1:2 * pair_count:2]].add(-swing)
    tile_counts = tile_counts + adjusted
    longest_at = jax.random.randint(key_longest, (), 0, DOCS).astype(jnp.int32)
    doc_index = jnp.arange(DOCS, dtype=jnp.int32)
    from_index = jnp.clip(jnp.where(doc_index < longest_at, doc_index, doc_index - 1), 0, other_docs - 1)
    tile_lengths = jnp.where(doc_index == longest_at, N_SEQ, tile_counts[from_index])
    return (tile_lengths * TILE).astype(jnp.int32)


def steps_of(own_key, shape, cuts, low, high):
    loudness, own = 1.0, jax.random.fold_in(own_key, 6)
    for dim, shards_of in cuts:
        heights = jnp.exp(jax.random.uniform(jax.random.fold_in(own, dim), (shards_of,), jnp.float32, low / len(cuts), high / len(cuts)))
        loudness = loudness * jnp.repeat(heights, shape[dim] // shards_of).reshape([-1 if axis == dim else 1 for axis in range(len(shape))])
    return loudness


def scatter_about(rng, dims, width, most, pieces=(), held_as=jnp.bfloat16):
    factor_of = steps_of(rng, dims, pieces, -0.22, 0.18) if pieces else 1.0
    values = jax.random.normal(rng, dims, jnp.float32) * width * factor_of
    return jnp.minimum(jnp.maximum(values, -most), most).astype(held_as)


def setup_inputs(seed: int = 0, part: int = 0) -> dict:
    splits = jax.random.split(jax.random.key(seed), 6)
    part_splits = jax.random.split(jax.random.fold_in(splits[5], part), 6)
    queries = draw_queries(jax.random.fold_in(jax.random.fold_in(splits[5], part), 71), part)
    keys = draw_keys(jax.random.fold_in(jax.random.fold_in(splits[5], part), 71), part)
    values = scatter_about(part_splits[2], (ROUNDS, BAND, WIDTH), 1.0, 6.0, ((1, 32),))
    cotangent = scatter_about(part_splits[3], (ROUNDS, BAND, WIDTH), 1.0, 6.0, ((1, 32),))
    lengths = draw_lengths(jax.random.fold_in(jax.random.fold_in(splits[5], part), 71), part)
    return dict(queries=queries, keys=keys, values=values, cotangent=cotangent, lengths=lengths)


def head_grads(blocks, allowed):
    query_rows = blocks[0]
    key_rows = blocks[1]
    value_rows = blocks[2]
    cot_rows = blocks[3]
    score_scale = 1.0 / math.sqrt(query_rows.shape[-1])
    scores = jnp.dot(query_rows, key_rows.T, preferred_element_type=jnp.float32) * score_scale
    scores = jnp.where(allowed, scores, -1e+30)
    row_max = lax.optimization_barrier(jnp.max(scores, axis=1, keepdims=True))
    weights = jnp.where(allowed, jnp.exp(scores - row_max), 0.0)
    denominator = lax.optimization_barrier(jnp.sum(weights, axis=1, keepdims=True))
    denominator = jnp.where(denominator > 0.0, denominator, 1.0)
    probs = weights / denominator
    probs_low = probs.astype(jnp.bfloat16)
    output = jnp.dot(probs_low, value_rows, preferred_element_type=jnp.float32)
    row_delta = lax.optimization_barrier(jnp.sum(cot_rows.astype(jnp.float32) * output, axis=1, keepdims=True))
    grad_probs = jnp.dot(cot_rows, value_rows.T, preferred_element_type=jnp.float32)
    grad_scores = (probs * (grad_probs - row_delta)).astype(jnp.bfloat16)
    grad_query = jnp.dot(grad_scores, key_rows, preferred_element_type=jnp.float32) * score_scale
    grad_key = jnp.dot(grad_scores.T, query_rows, preferred_element_type=jnp.float32) * score_scale
    grad_value = jnp.dot(probs_low.T, cot_rows, preferred_element_type=jnp.float32)
    return jnp.stack([grad_query, grad_key, grad_value]).astype(jnp.bfloat16)

def slot_grads(window, valid):
    band_rows = window.shape[0]
    full_width = window.shape[-1]
    allowed = valid[:, None] & valid[None, :]
    per_head = window.reshape(band_rows, 4, HEADS, HEAD_DIM).transpose(2, 1, 0, 3)
    result = lax.map(lambda blocks: head_grads(blocks, allowed), per_head)
    result = result.transpose(2, 1, 0, 3).reshape(band_rows, 3, full_width)
    return jnp.where(valid[:, None, None], result, jnp.zeros((), jnp.bfloat16))

def reference(queries, keys, values, cotangent, lengths):
    flat = jnp.stack([queries, keys, values, cotangent], axis=2).reshape(TOKENS, 4, WIDTH)
    padded = jnp.pad(flat, ((0, BAND), (0, 0), (0, 0)))
    starts = (jnp.cumsum(lengths) - lengths).astype(jnp.int32)

    def one_doc(doc_number, buffer):
        begin = starts[doc_number].astype(jnp.int32)
        length = lengths[doc_number].astype(jnp.int32)
        window = lax.dynamic_slice_in_dim(padded, begin, BAND, 0)
        valid = jnp.arange(BAND, dtype=jnp.int32) < length
        gradients = slot_grads(window, valid)
        previous = lax.dynamic_slice_in_dim(buffer, begin, BAND, 0)
        merged = jnp.where(valid[:, None, None], gradients, previous)
        return lax.dynamic_update_slice_in_dim(buffer, merged, begin, 0)
    buffer = lax.fori_loop(0, DOCS, one_doc, jnp.zeros((TOKENS + BAND, 3, WIDTH), jnp.bfloat16))
    result = buffer[:TOKENS].reshape(ROUNDS, BAND, 3, WIDTH)
    return (result[:, :, 0], result[:, :, 1], result[:, :, 2])
```

```python
import functools
import math

import jax
import jax.numpy as jnp
from jax import lax
from jax.experimental import pallas as pl
from jax.experimental.pallas import tpu as pltpu
from jax.sharding import PartitionSpec as P

HEAD_DIM = 128
TILE = 16
SUB = 256
FAR = -1e30
MESH = pl.DeviceIdType.MESH
STEPS = (
    (1, 0), (0, 1), (3, 0), (0, 3), (1, 1), (3, 3), (2, 0), (0, 2),
    (1, 3), (3, 1), (2, 2), (2, 1), (1, 2), (2, 3), (3, 2), (0, 0),
)
PEERS = tuple((dx, dy, dc) for dx, dy in STEPS for dc in (0, 1) if (dx, dy, dc) != (0, 0, 0))
PIECE = 2
PIECES = 7
HALF = PIECE * PIECES
SLOTS = HALF + 1
SUBS = 2 * SLOTS
WINDOW = 5


def first_round(core, piece):
    return core * (HALF + PIECE * piece) + (1 - core) * (HALF - PIECE - PIECE * piece)


def first_slot(core, piece):
    return first_round(core, piece) - core * (HALF - 1)


def kernel(
    queries, keys, values, cotangent, lens,
    grad_queries, grad_keys, grad_values,
    held, apart, member, sum_keys, sum_values, staged,
    in_sent, in_came, halo_sent, halo_came, out_sent, out_came,
):
    me = lax.axis_index("seq")
    chip_y, chip_x, core = me // 8, lax.rem(me // 2, 4), lax.rem(me, 2)
    chip = me // 2
    other = chip * 2 + 1 - core
    sources = (queries, keys, values, cotangent)
    results = (grad_queries, grad_keys, grad_values)

    def target(step):
        dx, dy, dc = step
        to_chip = lax.rem(chip_y + dy, 4) * 4 + lax.rem(chip_x + dx, 4)
        return to_chip, lax.rem(core + dc, 2)

    def head_columns(of_chip):
        return pl.ds(pl.multiple_of(of_chip * HEAD_DIM, HEAD_DIM), HEAD_DIM)

    def tile_rows(device):
        return pl.ds(pl.multiple_of(device * TILE, TILE), TILE)

    def block_rows(n):
        return n // 2, pl.ds(pl.multiple_of(lax.rem(n, 2) * SUB, SUB), SUB)

    barrier = pltpu.get_barrier_semaphore()

    def greet(i, carry):
        pl.semaphore_signal(
            barrier, inc=1, device_id={"seq": lax.rem(me + i, 32)}, device_id_type=MESH
        )
        return carry

    lax.fori_loop(1, 32, greet, 0)

    def send_in(piece):
        for a, source in enumerate(sources):
            pltpu.make_async_copy(
                source.at[pl.ds(first_round(core, piece), PIECE), :, head_columns(chip)],
                held.at[a, pl.ds(first_slot(core, piece), PIECE), tile_rows(me), :],
                in_came.at[piece],
            ).start()
            for step in PEERS:
                to_chip, to_core = target(step)
                pltpu.make_async_remote_copy(
                    source.at[pl.ds(first_round(to_core, piece), PIECE), :, head_columns(to_chip)],
                    held.at[a, pl.ds(first_slot(to_core, piece), PIECE), tile_rows(me), :],
                    in_sent,
                    in_came.at[piece],
                    device_id={"seq": to_chip * 2 + to_core},
                    device_id_type=MESH,
                ).start()

    def send_out(piece):
        for a, result in enumerate(results):
            rounds = pl.ds(first_round(core, piece), PIECE)
            slots = pl.ds(first_slot(core, piece), PIECE)
            pltpu.make_async_copy(
                staged.at[a, slots, tile_rows(me), :],
                result.at[rounds, :, head_columns(chip)],
                out_came.at[a],
            ).start()
            for step in PEERS:
                to_chip, to_core = target(step)
                to = to_chip * 2 + to_core
                pltpu.make_async_remote_copy(
                    staged.at[a, slots, tile_rows(to), :],
                    result.at[rounds, :, head_columns(chip)],
                    out_sent,
                    out_came.at[a],
                    device_id={"seq": to},
                    device_id_type=MESH,
                ).start()

    before = lax.broadcasted_iota(jnp.int32, (HEAD_DIM, HEAD_DIM), 0) < lax.broadcasted_iota(
        jnp.int32, (HEAD_DIM, HEAD_DIM), 1
    )
    starts = jnp.dot(
        lens[...],
        jnp.where(before, 1.0, 0.0).astype(jnp.bfloat16),
        preferred_element_type=jnp.float32,
    )[0:1, :].astype(jnp.int32)
    ends = starts + lens[...].astype(jnp.float32)[0:1, :].astype(jnp.int32)

    def mark(n, carry):
        token = core * (HALF - 1) * 2 * SUB + n * SUB
        token = token + lax.broadcasted_iota(jnp.int32, (SUB, HEAD_DIM), 0)
        inside = (token >= starts) & (token < ends)
        place = block_rows(n)
        apart[*place] = jnp.where(inside, 0.0, FAR).astype(jnp.bfloat16)
        member[*place] = jnp.where(inside, 1.0, 0.0).astype(jnp.bfloat16)
        zeros = jnp.zeros((SUB, HEAD_DIM), jnp.float32)
        sum_keys[*place] = zeros
        sum_values[*place] = zeros
        return carry

    pl.semaphore_wait(barrier, 31)

    def send_piece(piece, carry):
        send_in(piece)
        return carry

    lax.fori_loop(0, PIECES, send_piece, 0)
    lax.fori_loop(0, SUBS, mark, 0)

    scale = 1.0 / math.sqrt(HEAD_DIM)
    log_scale = scale * math.log2(math.e)
    across = (((1,), (1,)), ((), ()))
    down = (((0,), (0,)), ((), ()))

    def attend(t):
        n = core * t + (1 - core) * (SUBS - 1 - t)
        first = jnp.clip(n - WINDOW // 2, 0, SUBS - WINDOW)
        here = block_rows(n)
        q_rows, c_rows = held[0, *here], held[3, *here]
        q_wide = jnp.concatenate([q_rows, apart[*here]], axis=1)
        places = [block_rows(first + i) for i in range(WINDOW)]
        scores = []
        for place in places:
            k_wide = jnp.concatenate([held[1, *place], member[*place]], axis=1)
            scores.append(
                lax.dot_general(k_wide, q_wide, across, preferred_element_type=jnp.float32)
            )
        top = functools.reduce(jnp.maximum, [jnp.max(s, axis=0, keepdims=True) for s in scores])
        top = top * log_scale
        weights = [jnp.exp2(s * log_scale - top) for s in scores]
        total = sum(jnp.sum(w, axis=0, keepdims=True) for w in weights)
        share = 1.0 / total
        probs = [w * share for w in weights]
        grad_probs = [
            lax.dot_general(held[2, *place], c_rows, across, preferred_element_type=jnp.float32)
            for place in places
        ]
        delta = sum(
            jnp.sum(p * g, axis=0, keepdims=True) for p, g in zip(probs, grad_probs, strict=True)
        )
        grad_q = jnp.zeros((SUB, HEAD_DIM), jnp.float32)
        for place, p, g in zip(places, probs, grad_probs, strict=True):
            grad_s = (p * (g - delta)).astype(jnp.bfloat16)
            sum_values[*place] += jnp.dot(
                p.astype(jnp.bfloat16), c_rows, preferred_element_type=jnp.float32
            )
            sum_keys[*place] += jnp.dot(grad_s, q_rows, preferred_element_type=jnp.float32)
            grad_q += lax.dot_general(
                grad_s, held[1, *place], down, preferred_element_type=jnp.float32
            )
        staged[0, *here] = (grad_q * scale).astype(jnp.bfloat16)

    def round_off(piece):
        def one(i, carry):
            place = block_rows(2 * first_slot(core, piece) + i)
            staged[1, *place] = (sum_keys[*place] * scale).astype(jnp.bfloat16)
            staged[2, *place] = sum_values[*place].astype(jnp.bfloat16)
            return carry

        lax.fori_loop(0, 2 * PIECE, one, 0)

    def beyond(side_sent, side_came):
        return pltpu.make_async_remote_copy(
            held.at[:, side_sent],
            held.at[:, side_came],
            halo_sent,
            halo_came,
            device_id={"seq": other},
            device_id_type=MESH,
        )

    per_piece = 2 * PIECE

    def step(t, carry):
        @pl.when((lax.rem(t, per_piece) == 0) & (t < PIECES * per_piece))
        def _():
            piece = t // per_piece
            arrived = held.at[:, pl.ds(first_slot(core, piece), PIECE)]
            pltpu.make_async_copy(arrived, arrived, in_came.at[piece]).wait()

        @pl.when(t == 0)
        def _():
            halo = beyond(core + (1 - core) * (HALF - 1), (1 - core) * 0 + core * HALF)
            halo.start()
            halo.wait()

        attend(t)
        last = t == SUBS - 1

        @pl.when(((lax.rem(t, per_piece) == per_piece - 1) & (t >= 2 * per_piece - 1)) | last)
        def _():
            piece = jnp.where(last, PIECES - 1, (t - (per_piece - 1)) // per_piece - 1)
            round_off(piece)
            send_out(piece)

        return carry

    lax.fori_loop(0, SUBS, step, 0)

    for a, result in enumerate(results):
        pltpu.make_async_copy(result, result, out_came.at[a]).wait()
    most = pl.ds(0, 31 * TILE)
    left = held.at[:, pl.ds(0, HALF), most, :]
    pltpu.make_async_copy(left, left, in_sent).wait()
    left = staged.at[:, pl.ds(0, HALF), most, :]
    pltpu.make_async_copy(left, left, out_sent).wait()


def per_device(queries, keys, values, cotangent, lengths):
    lens = jnp.pad(lengths, (0, HEAD_DIM - lengths.shape[0])).astype(jnp.bfloat16)
    lens = jnp.broadcast_to(lens[None], (TILE, HEAD_DIM))
    anywhere = pl.BlockSpec(memory_space=pl.ANY)
    block = (SLOTS, 2 * SUB, HEAD_DIM)
    return pl.pallas_call(
        kernel,
        out_shape=[jax.ShapeDtypeStruct(queries.shape, jnp.bfloat16)] * 3,
        in_specs=[anywhere] * 4 + [pl.BlockSpec(memory_space=pltpu.VMEM)],
        out_specs=[anywhere] * 3,
        scratch_shapes=[
            pltpu.VMEM((4, *block), jnp.bfloat16),
            pltpu.VMEM(block, jnp.bfloat16),
            pltpu.VMEM(block, jnp.bfloat16),
            pltpu.VMEM(block, jnp.float32),
            pltpu.VMEM(block, jnp.float32),
            pltpu.VMEM((3, *block), jnp.bfloat16),
            pltpu.SemaphoreType.DMA,
            pltpu.SemaphoreType.DMA((PIECES,)),
            pltpu.SemaphoreType.DMA,
            pltpu.SemaphoreType.DMA,
            pltpu.SemaphoreType.DMA,
            pltpu.SemaphoreType.DMA((3,)),
        ],
        compiler_params=pltpu.CompilerParams(
            collective_id=0, has_side_effects=True, vmem_limit_bytes=56 * 2**20
        ),
        name="attention_grads",
    )(queries, keys, values, cotangent, lens)


def solution(mesh):
    rows = P(None, ("grp", "seq"), None)
    return jax.shard_map(
        per_device,
        mesh=mesh,
        in_specs=(rows, rows, rows, rows, P("grp")),
        out_specs=(rows, rows, rows),
        check_vma=False,
    )
```

```python
import functools
import math

import jax
import jax.numpy as jnp
from jax import lax
from jax.experimental import pallas as pl
from jax.experimental.pallas import tpu as pltpu
from jax.sharding import PartitionSpec as P

HEAD_DIM = 128
TILE = 16
SUB = 256
FAR = -1e30
MESH = pl.DeviceIdType.MESH
STEPS = (
    (1, 0), (0, 1), (3, 0), (0, 3), (1, 1), (3, 3), (2, 0), (0, 2),
    (1, 3), (3, 1), (2, 2), (2, 1), (1, 2), (2, 3), (3, 2), (0, 0),
)
PEERS = tuple((dx, dy, dc) for dx, dy in STEPS for dc in (0, 1) if (dx, dy, dc) != (0, 0, 0))
PIECE = 2
PIECES = 7
HALF = PIECE * PIECES
SLOTS = HALF + 1
SUBS = 2 * SLOTS
PART = 7
WINDOW = 5


def first_round(core, piece):
    return core * (HALF + PIECE * piece) + (1 - core) * (HALF - PIECE - PIECE * piece)


def first_slot(core, piece):
    return first_round(core, piece) - core * (HALF - 1)


def kernel(
    queries, keys, values, cotangent, lens,
    grad_queries, grad_keys, grad_values,
    held, apart, member, sum_keys, sum_values, staged,
    in_sent, in_came, halo_sent, halo_came, out_sent, out_came,
):
    me = lax.axis_index("seq")
    chip_y, chip_x, core = me // 8, lax.rem(me // 2, 4), lax.rem(me, 2)
    chip = me // 2
    other = chip * 2 + 1 - core
    sources = (queries, keys, values, cotangent)
    results = (grad_queries, grad_keys, grad_values)

    def target(step):
        dx, dy, dc = step
        to_chip = lax.rem(chip_y + dy, 4) * 4 + lax.rem(chip_x + dx, 4)
        return to_chip, lax.rem(core + dc, 2)

    def head_columns(of_chip):
        return pl.ds(pl.multiple_of(of_chip * HEAD_DIM, HEAD_DIM), HEAD_DIM)

    def tile_rows(device):
        return pl.ds(pl.multiple_of(device * TILE, TILE), TILE)

    def block_rows(n):
        return n // 2, pl.ds(pl.multiple_of(lax.rem(n, 2) * SUB, SUB), SUB)

    barrier = pltpu.get_barrier_semaphore()

    def greet(i, carry):
        pl.semaphore_signal(
            barrier, inc=1, device_id={"seq": lax.rem(me + i, 32)}, device_id_type=MESH
        )
        return carry

    lax.fori_loop(1, 32, greet, 0)

    def send_in(piece):
        for a, source in enumerate(sources):
            pltpu.make_async_copy(
                source.at[pl.ds(first_round(core, piece), PIECE), :, head_columns(chip)],
                held.at[a, pl.ds(first_slot(core, piece), PIECE), tile_rows(me), :],
                in_came.at[piece],
            ).start()
            for step in PEERS:
                to_chip, to_core = target(step)
                pltpu.make_async_remote_copy(
                    source.at[pl.ds(first_round(to_core, piece), PIECE), :, head_columns(to_chip)],
                    held.at[a, pl.ds(first_slot(to_core, piece), PIECE), tile_rows(me), :],
                    in_sent,
                    in_came.at[piece],
                    device_id={"seq": to_chip * 2 + to_core},
                    device_id_type=MESH,
                ).start()

    def send_out(piece):
        for a, result in enumerate(results):
            rounds = pl.ds(first_round(core, piece), PIECE)
            slots = pl.ds(first_slot(core, piece), PIECE)
            pltpu.make_async_copy(
                staged.at[a, slots, tile_rows(me), :],
                result.at[rounds, :, head_columns(chip)],
                out_came.at[a],
            ).start()
            for step in PEERS:
                to_chip, to_core = target(step)
                to = to_chip * 2 + to_core
                pltpu.make_async_remote_copy(
                    staged.at[a, slots, tile_rows(to), :],
                    result.at[rounds, :, head_columns(chip)],
                    out_sent,
                    out_came.at[a],
                    device_id={"seq": to},
                    device_id_type=MESH,
                ).start()

    before = lax.broadcasted_iota(jnp.int32, (HEAD_DIM, HEAD_DIM), 0) < lax.broadcasted_iota(
        jnp.int32, (HEAD_DIM, HEAD_DIM), 1
    )
    starts = jnp.dot(
        lens[...],
        jnp.where(before, 1.0, 0.0).astype(jnp.bfloat16),
        preferred_element_type=jnp.float32,
    )[0:1, :].astype(jnp.int32)
    ends = starts + lens[...].astype(jnp.float32)[0:1, :].astype(jnp.int32)

    def mark(n, carry):
        token = core * (HALF - 1) * 2 * SUB + n * SUB
        token = token + lax.broadcasted_iota(jnp.int32, (SUB, HEAD_DIM), 0)
        inside = (token >= starts) & (token < ends)
        place = block_rows(n)
        apart[*place] = jnp.where(inside, 0.0, FAR).astype(jnp.bfloat16)
        member[*place] = jnp.where(inside, 1.0, 0.0).astype(jnp.bfloat16)
        zeros = jnp.zeros((SUB, HEAD_DIM), jnp.float32)
        sum_keys[*place] = zeros
        sum_values[*place] = zeros
        return carry

    pl.semaphore_wait(barrier, 31)

    def send_piece(piece, carry):
        send_in(piece)
        return carry

    lax.fori_loop(0, PIECES, send_piece, 0)
    lax.fori_loop(0, SUBS, mark, 0)

    scale = 1.0 / math.sqrt(HEAD_DIM)
    log_scale = scale * math.log2(math.e)
    across = (((1,), (1,)), ((), ()))
    down = (((0,), (0,)), ((), ()))

    def attend(t):
        n = core * t + (1 - core) * (SUBS - 1 - t)
        first = jnp.clip(n - WINDOW // 2, 0, SUBS - WINDOW)
        here = block_rows(n)
        q_rows, c_rows = held[0, *here], held[3, *here]
        q_wide = jnp.concatenate([q_rows, apart[*here]], axis=1)
        places = [block_rows(first + i) for i in range(WINDOW)]
        scores = []
        for place in places:
            k_wide = jnp.concatenate([held[1, *place], member[*place]], axis=1)
            scores.append(
                lax.dot_general(k_wide, q_wide, across, preferred_element_type=jnp.float32)
            )
        top = functools.reduce(jnp.maximum, [jnp.max(s, axis=0, keepdims=True) for s in scores])
        top = top * log_scale
        weights = [jnp.exp2(s * log_scale - top) for s in scores]
        total = sum(jnp.sum(w, axis=0, keepdims=True) for w in weights)
        share = 1.0 / total
        probs = [w * share for w in weights]
        grad_probs = [
            lax.dot_general(held[2, *place], c_rows, across, preferred_element_type=jnp.float32)
            for place in places
        ]
        delta = sum(
            jnp.sum(p * g, axis=0, keepdims=True) for p, g in zip(probs, grad_probs, strict=True)
        )
        grad_q = jnp.zeros((SUB, HEAD_DIM), jnp.float32)
        for place, p, g in zip(places, probs, grad_probs, strict=True):
            grad_s = (p * (g - delta)).astype(jnp.bfloat16)
            sum_values[*place] += jnp.dot(
                p.astype(jnp.bfloat16), c_rows, preferred_element_type=jnp.float32
            )
            sum_keys[*place] += jnp.dot(grad_s, q_rows, preferred_element_type=jnp.float32)
            grad_q += lax.dot_general(
                grad_s, held[1, *place], down, preferred_element_type=jnp.float32
            )
        staged[0, *here] = (grad_q * scale).astype(jnp.bfloat16)

    def round_off(piece):
        def one(i, carry):
            place = block_rows(2 * first_slot(core, piece) + i)
            staged[1, *place] = (sum_keys[*place] * scale).astype(jnp.bfloat16)
            staged[2, *place] = sum_values[*place].astype(jnp.bfloat16)
            return carry

        lax.fori_loop(0, 2 * PIECE, one, 0)

    def beyond(side_sent, side_came):
        return pltpu.make_async_remote_copy(
            held.at[:, side_sent],
            held.at[:, side_came],
            halo_sent,
            halo_came,
            device_id={"seq": other},
            device_id_type=MESH,
        )

    per_piece = 2 * PIECE

    def step(t, carry):
        @pl.when((lax.rem(t, per_piece) == 0) & (t < PIECES * per_piece))
        def _():
            piece = t // per_piece
            arrived = held.at[:, pl.ds(first_slot(core, piece), PIECE)]
            pltpu.make_async_copy(arrived, arrived, in_came.at[piece]).wait()

        @pl.when(t == 0)
        def _():
            halo = beyond(core + (1 - core) * (HALF - 1), (1 - core) * 0 + core * HALF)
            halo.start()
            halo.wait()

        attend(t)
        last = t == SUBS - 1

        @pl.when(((lax.rem(t, per_piece) == per_piece - 1) & (t >= 2 * per_piece - 1)) | last)
        def _():
            piece = jnp.where(last, PIECES - 1, (t - (per_piece - 1)) // per_piece - 1)
            round_off(piece)
            send_out(piece)

        return carry

    lax.fori_loop(0, SUBS, step, 0)

    for a, result in enumerate(results):
        pltpu.make_async_copy(result, result, out_came.at[a]).wait()
    most = pl.ds(0, 31 * TILE)
    left = held.at[:, pl.ds(0, HALF), most, :]
    pltpu.make_async_copy(left, left, in_sent).wait()
    left = staged.at[:, pl.ds(0, HALF), most, :]
    pltpu.make_async_copy(left, left, out_sent).wait()


def write_out(*refs):
    sources, results, (held, came, sent) = refs[:3], refs[3:6], refs[6:]

    def part(ref, i):
        return ref.at[pl.ds(PART * i, PART)]

    def fetch(a, i):
        return pltpu.make_async_copy(part(sources[a], i), part(held.at[a], i), came.at[a, i])

    def store(a, i):
        return pltpu.make_async_copy(part(held.at[a], i), part(results[a], i), sent.at[a, i])

    order = [(a, i) for i in range(results[0].shape[0] // PART) for a in range(3)]
    for place in order:
        fetch(*place).start()
    for place in order:
        fetch(*place).wait()
        store(*place).start()
    for place in order:
        store(*place).wait()


def per_device(queries, keys, values, cotangent, lengths):
    lens = jnp.pad(lengths, (0, HEAD_DIM - lengths.shape[0])).astype(jnp.bfloat16)
    lens = jnp.broadcast_to(lens[None], (TILE, HEAD_DIM))
    anywhere = pl.BlockSpec(memory_space=pl.ANY)
    block = (SLOTS, 2 * SUB, HEAD_DIM)
    parts = queries.shape[0] // PART
    grads = pl.pallas_call(
        kernel,
        out_shape=[jax.ShapeDtypeStruct(queries.shape, jnp.bfloat16)] * 3,
        in_specs=[anywhere] * 4 + [pl.BlockSpec(memory_space=pltpu.VMEM)],
        out_specs=[anywhere] * 3,
        scratch_shapes=[
            pltpu.VMEM((4, *block), jnp.bfloat16),
            pltpu.VMEM(block, jnp.bfloat16),
            pltpu.VMEM(block, jnp.bfloat16),
            pltpu.VMEM(block, jnp.float32),
            pltpu.VMEM(block, jnp.float32),
            pltpu.VMEM((3, *block), jnp.bfloat16),
            pltpu.SemaphoreType.DMA,
            pltpu.SemaphoreType.DMA((PIECES,)),
            pltpu.SemaphoreType.DMA,
            pltpu.SemaphoreType.DMA,
            pltpu.SemaphoreType.DMA,
            pltpu.SemaphoreType.DMA((3,)),
        ],
        compiler_params=pltpu.CompilerParams(
            collective_id=0, has_side_effects=True, vmem_limit_bytes=56 * 2**20
        ),
        name="attention_grads",
    )(queries, keys, values, cotangent, lens)
    return pl.pallas_call(
        write_out,
        out_shape=[jax.ShapeDtypeStruct(queries.shape, jnp.bfloat16)] * 3,
        in_specs=[anywhere] * 3,
        out_specs=[anywhere] * 3,
        scratch_shapes=[
            pltpu.VMEM((3, *queries.shape), jnp.bfloat16),
            pltpu.SemaphoreType.DMA((3, parts)),
            pltpu.SemaphoreType.DMA((3, parts)),
        ],
        compiler_params=pltpu.CompilerParams(vmem_limit_bytes=56 * 2**20),
        name="write_out",
    )(*grads)


def solution(mesh):
    rows = P(None, ("grp", "seq"), None)
    return jax.shard_map(
        per_device,
        mesh=mesh,
        in_specs=(rows, rows, rows, rows, P("grp")),
        out_specs=(rows, rows, rows),
        check_vma=False,
    )
```

```python
import functools
import math

import jax
import jax.numpy as jnp
from jax import lax
from jax.experimental import pallas as pl
from jax.experimental.pallas import tpu as pltpu
from jax.sharding import PartitionSpec as P

HEAD_DIM = 128
TILE = 16
SUB = 256
FAR = -1e30
MESH = pl.DeviceIdType.MESH
STEPS = (
    (1, 0), (0, 1), (3, 0), (0, 3), (1, 1), (3, 3), (2, 0), (0, 2),
    (1, 3), (3, 1), (2, 2), (2, 1), (1, 2), (2, 3), (3, 2), (0, 0),
)
PEERS = tuple((dx, dy, dc) for dx, dy in STEPS for dc in (0, 1) if (dx, dy, dc) != (0, 0, 0))
PIECE = 2
PIECES = 7
HALF = PIECE * PIECES
SLOTS = HALF + 1
SUBS = 2 * SLOTS
PART = 7
WINDOW = 5


def first_round(core, piece):
    return core * (HALF + PIECE * piece) + (1 - core) * (HALF - PIECE - PIECE * piece)


def first_slot(core, piece):
    return first_round(core, piece) - core * (HALF - 1)


def kernel(
    queries, keys, values, cotangent, lens,
    grad_queries, grad_keys, grad_values,
    held, apart, member, sum_keys, sum_values, staged,
    in_sent, in_came, halo_sent, halo_came, out_sent, out_came,
):
    me = lax.axis_index("seq")
    chip_y, chip_x, core = me // 8, lax.rem(me // 2, 4), lax.rem(me, 2)
    chip = me // 2
    other = chip * 2 + 1 - core
    sources = (queries, keys, values, cotangent)
    results = (grad_queries, grad_keys, grad_values)

    def target(step):
        dx, dy, dc = step
        to_chip = lax.rem(chip_y + dy, 4) * 4 + lax.rem(chip_x + dx, 4)
        return to_chip, lax.rem(core + dc, 2)

    def head_columns(of_chip):
        return pl.ds(pl.multiple_of(of_chip * HEAD_DIM, HEAD_DIM), HEAD_DIM)

    def tile_rows(device):
        return pl.ds(pl.multiple_of(device * TILE, TILE), TILE)

    def block_rows(n):
        return n // 2, pl.ds(pl.multiple_of(lax.rem(n, 2) * SUB, SUB), SUB)

    barrier = pltpu.get_barrier_semaphore()

    def greet(i, carry):
        pl.semaphore_signal(
            barrier, inc=1, device_id={"seq": lax.rem(me + i, 32)}, device_id_type=MESH
        )
        return carry

    lax.fori_loop(1, 32, greet, 0)

    def send_in(piece):
        for a, source in enumerate(sources):
            pltpu.make_async_copy(
                source.at[pl.ds(first_round(core, piece), PIECE), :, head_columns(chip)],
                held.at[a, pl.ds(first_slot(core, piece), PIECE), tile_rows(me), :],
                in_came.at[piece],
            ).start()
            for step in PEERS:
                to_chip, to_core = target(step)
                pltpu.make_async_remote_copy(
                    source.at[pl.ds(first_round(to_core, piece), PIECE), :, head_columns(to_chip)],
                    held.at[a, pl.ds(first_slot(to_core, piece), PIECE), tile_rows(me), :],
                    in_sent,
                    in_came.at[piece],
                    device_id={"seq": to_chip * 2 + to_core},
                    device_id_type=MESH,
                ).start()

    def send_out(piece):
        for a, result in enumerate(results):
            rounds = pl.ds(first_round(core, piece), PIECE)
            slots = pl.ds(first_slot(core, piece), PIECE)
            pltpu.make_async_copy(
                staged.at[a, slots, tile_rows(me), :],
                result.at[rounds, :, head_columns(chip)],
                out_came.at[a],
            ).start()
            for step in PEERS:
                to_chip, to_core = target(step)
                to = to_chip * 2 + to_core
                pltpu.make_async_remote_copy(
                    staged.at[a, slots, tile_rows(to), :],
                    result.at[rounds, :, head_columns(chip)],
                    out_sent,
                    out_came.at[a],
                    device_id={"seq": to},
                    device_id_type=MESH,
                ).start()

    table = (lens.shape[1], HEAD_DIM)
    row = lax.broadcasted_iota(jnp.int32, table, 0)
    column = lax.broadcasted_iota(jnp.int32, table, 1)
    sizes = jnp.broadcast_to(lens[...].astype(jnp.float32), (TILE, table[0])).astype(jnp.bfloat16)

    def total(chosen):
        chosen = jnp.where(chosen, 1.0, 0.0).astype(jnp.bfloat16)
        return jnp.dot(sizes, chosen, preferred_element_type=jnp.float32)[0:1, :].astype(jnp.int32)

    starts, ends = total(row < column), total(row <= column)

    def mark(n, carry):
        token = core * (HALF - 1) * 2 * SUB + n * SUB
        token = token + lax.broadcasted_iota(jnp.int32, (SUB, HEAD_DIM), 0)
        inside = (token >= starts) & (token < ends)
        place = block_rows(n)
        apart[*place] = jnp.where(inside, 0.0, FAR).astype(jnp.bfloat16)
        member[*place] = jnp.where(inside, 1.0, 0.0).astype(jnp.bfloat16)
        zeros = jnp.zeros((SUB, HEAD_DIM), jnp.float32)
        sum_keys[*place] = zeros
        sum_values[*place] = zeros
        return carry

    pl.semaphore_wait(barrier, 31)

    def send_piece(piece, carry):
        send_in(piece)
        return carry

    lax.fori_loop(0, PIECES, send_piece, 0)
    lax.fori_loop(0, SUBS, mark, 0)

    scale = 1.0 / math.sqrt(HEAD_DIM)
    log_scale = scale * math.log2(math.e)
    across = (((1,), (1,)), ((), ()))
    down = (((0,), (0,)), ((), ()))

    def attend(t):
        n = core * t + (1 - core) * (SUBS - 1 - t)
        first = jnp.clip(n - WINDOW // 2, 0, SUBS - WINDOW)
        here = block_rows(n)
        q_rows, c_rows = held[0, *here], held[3, *here]
        q_wide = jnp.concatenate([q_rows, apart[*here]], axis=1)
        places = [block_rows(first + i) for i in range(WINDOW)]
        scores = []
        for place in places:
            k_wide = jnp.concatenate([held[1, *place], member[*place]], axis=1)
            scores.append(
                lax.dot_general(k_wide, q_wide, across, preferred_element_type=jnp.float32)
            )
        top = functools.reduce(jnp.maximum, [jnp.max(s, axis=0, keepdims=True) for s in scores])
        top = top * log_scale
        weights = [jnp.exp2(s * log_scale - top) for s in scores]
        total = sum(jnp.sum(w, axis=0, keepdims=True) for w in weights)
        share = 1.0 / total
        probs = [w * share for w in weights]
        grad_probs = [
            lax.dot_general(held[2, *place], c_rows, across, preferred_element_type=jnp.float32)
            for place in places
        ]
        delta = sum(
            jnp.sum(p * g, axis=0, keepdims=True) for p, g in zip(probs, grad_probs, strict=True)
        )
        grad_q = jnp.zeros((SUB, HEAD_DIM), jnp.float32)
        for place, p, g in zip(places, probs, grad_probs, strict=True):
            grad_s = (p * (g - delta)).astype(jnp.bfloat16)
            sum_values[*place] += jnp.dot(
                p.astype(jnp.bfloat16), c_rows, preferred_element_type=jnp.float32
            )
            sum_keys[*place] += jnp.dot(grad_s, q_rows, preferred_element_type=jnp.float32)
            grad_q += lax.dot_general(
                grad_s, held[1, *place], down, preferred_element_type=jnp.float32
            )
        staged[0, *here] = (grad_q * scale).astype(jnp.bfloat16)

    def round_off(piece):
        def one(i, carry):
            place = block_rows(2 * first_slot(core, piece) + i)
            staged[1, *place] = (sum_keys[*place] * scale).astype(jnp.bfloat16)
            staged[2, *place] = sum_values[*place].astype(jnp.bfloat16)
            return carry

        lax.fori_loop(0, 2 * PIECE, one, 0)

    def beyond(side_sent, side_came):
        return pltpu.make_async_remote_copy(
            held.at[:, side_sent],
            held.at[:, side_came],
            halo_sent,
            halo_came,
            device_id={"seq": other},
            device_id_type=MESH,
        )

    per_piece = 2 * PIECE

    def step(t, carry):
        @pl.when((lax.rem(t, per_piece) == 0) & (t < PIECES * per_piece))
        def _():
            piece = t // per_piece
            arrived = held.at[:, pl.ds(first_slot(core, piece), PIECE)]
            pltpu.make_async_copy(arrived, arrived, in_came.at[piece]).wait()

        @pl.when(t == 0)
        def _():
            halo = beyond(core + (1 - core) * (HALF - 1), (1 - core) * 0 + core * HALF)
            halo.start()
            halo.wait()

        attend(t)
        last = t == SUBS - 1

        @pl.when(((lax.rem(t, per_piece) == per_piece - 1) & (t >= 2 * per_piece - 1)) | last)
        def _():
            piece = jnp.where(last, PIECES - 1, (t - (per_piece - 1)) // per_piece - 1)
            round_off(piece)
            send_out(piece)

        return carry

    lax.fori_loop(0, SUBS, step, 0)

    for a, result in enumerate(results):
        pltpu.make_async_copy(result, result, out_came.at[a]).wait()
    most = pl.ds(0, 31 * TILE)
    left = held.at[:, pl.ds(0, HALF), most, :]
    pltpu.make_async_copy(left, left, in_sent).wait()
    left = staged.at[:, pl.ds(0, HALF), most, :]
    pltpu.make_async_copy(left, left, out_sent).wait()


def write_out(*refs):
    sources, results, (held, came, sent) = refs[:3], refs[3:6], refs[6:]

    def part(ref, i):
        return ref.at[pl.ds(PART * i, PART)]

    def fetch(a, i):
        return pltpu.make_async_copy(part(sources[a], i), part(held.at[a], i), came.at[a, i])

    def store(a, i):
        return pltpu.make_async_copy(part(held.at[a], i), part(results[a], i), sent.at[a, i])

    order = [(a, i) for i in range(results[0].shape[0] // PART) for a in range(3)]
    for place in order:
        fetch(*place).start()
    for place in order:
        fetch(*place).wait()
        store(*place).start()
    for place in order:
        store(*place).wait()


def per_device(queries, keys, values, cotangent, lengths):
    anywhere = pl.BlockSpec(memory_space=pl.ANY)
    block = (SLOTS, 2 * SUB, HEAD_DIM)
    parts = queries.shape[0] // PART
    grads = pl.pallas_call(
        kernel,
        out_shape=[jax.ShapeDtypeStruct(queries.shape, jnp.bfloat16)] * 3,
        in_specs=[anywhere] * 4 + [pl.BlockSpec(memory_space=pltpu.VMEM)],
        out_specs=[anywhere] * 3,
        scratch_shapes=[
            pltpu.VMEM((4, *block), jnp.bfloat16),
            pltpu.VMEM(block, jnp.bfloat16),
            pltpu.VMEM(block, jnp.bfloat16),
            pltpu.VMEM(block, jnp.float32),
            pltpu.VMEM(block, jnp.float32),
            pltpu.VMEM((3, *block), jnp.bfloat16),
            pltpu.SemaphoreType.DMA,
            pltpu.SemaphoreType.DMA((PIECES,)),
            pltpu.SemaphoreType.DMA,
            pltpu.SemaphoreType.DMA,
            pltpu.SemaphoreType.DMA,
            pltpu.SemaphoreType.DMA((3,)),
        ],
        compiler_params=pltpu.CompilerParams(
            collective_id=0, has_side_effects=True, vmem_limit_bytes=56 * 2**20
        ),
        name="attention_grads",
    )(queries, keys, values, cotangent, lengths.reshape(1, -1))
    return pl.pallas_call(
        write_out,
        out_shape=[jax.ShapeDtypeStruct(queries.shape, jnp.bfloat16)] * 3,
        in_specs=[anywhere] * 3,
        out_specs=[anywhere] * 3,
        scratch_shapes=[
            pltpu.VMEM((3, *queries.shape), jnp.bfloat16),
            pltpu.SemaphoreType.DMA((3, parts)),
            pltpu.SemaphoreType.DMA((3, parts)),
        ],
        compiler_params=pltpu.CompilerParams(vmem_limit_bytes=56 * 2**20),
        name="write_out",
    )(*grads)


def solution(mesh):
    rows = P(None, ("grp", "seq"), None)
    return jax.shard_map(
        per_device,
        mesh=mesh,
        in_specs=(rows, rows, rows, rows, P("grp")),
        out_specs=(rows, rows, rows),
        check_vma=False,
    )
```
